32 devices in a mesh: batch: 16 (over z, y, x), tensor: 2 (over core).
Axes of the slice: x: 2, y: 2, z: 4, core: 2. Of those that a mesh axis runs over, the one named last changes fastest.
Arguments:
- block_in: bfloat16 [32768, 768], P(('batch', 'tensor')), may hold values from -6 to 6
- seq_len: int32 [16, 4], P('batch'), may hold values from 0 to 2048, as said below
- ln1_gain: bfloat16 [768], replicated, may hold values from 0.5 to 1.5
- ln1_bias: bfloat16 [768], replicated, may hold values from -3 to 3
- qkv_weight: bfloat16 [768, 3, 768], P(None, None, 'tensor'), may hold values from -0.21875 to 0.21875
- qkv_bias: bfloat16 [3, 768], P(None, 'tensor'), may hold values from -3 to 3
- out_weight: bfloat16 [768, 768], P('tensor'), may hold values from -1.25 to 1.25
- out_bias: bfloat16 [768], replicated, may hold values from -3 to 3
- ln2_gain: bfloat16 [768], replicated, may hold values from 0.5 to 1.5
- ln2_bias: bfloat16 [768], replicated, may hold values from -3 to 3
- fc_weight: bfloat16 [768, 3072], P(None, 'tensor'), may hold values from -0.21875 to 0.21875
- fc_bias: bfloat16 [3072], P('tensor'), may hold values from -3 to 3
- proj_weight: bfloat16 [3072, 768], P('tensor'), may hold values from -0.109375 to 0.109375
- proj_bias: bfloat16 [768], replicated, may hold values from -3 to 3
- cotangent: bfloat16 [32768, 768], P(('batch', 'tensor')), may hold values from -6 to 6
Outputs:
- block_out: bfloat16 [32768, 768], P(('batch', 'tensor'))
- input_grad: bfloat16 [32768, 768], P(('batch', 'tensor'))
- ln1_gain_grad: float32 [768], replicated
- ln1_bias_grad: float32 [768], replicated
- qkv_weight_grad: float32 [768, 3, 768], P(None, None, 'tensor')
- qkv_bias_grad: float32 [3, 768], P(None, 'tensor')
- out_weight_grad: float32 [768, 768], P('tensor')
- out_bias_grad: float32 [768], replicated
- ln2_gain_grad: float32 [768], replicated
- ln2_bias_grad: float32 [768], replicated
- fc_weight_grad: float32 [768, 3072], P(None, 'tensor')
- fc_bias_grad: float32 [3072], P('tensor')
- proj_weight_grad: float32 [3072, 768], P('tensor')
- proj_bias_grad: float32 [768], replicated
The draws below stay inside these ranges and needn't reach their ends.
Inputs may be any that keep to these rules, and one draw needn't show every extreme that they name: `seq_len`: each row lists the lengths of one batch group's sequences, nonzero ones first; every nonzero length is 512, 1024 or 2048, a row sums to at most 2048, and some row holds a sequence of 2048.
All inputs are finite; a program needn't handle non-finite values.
Results may differ from the reference program's by a relative error of at most 0.0097.
Values may be sent and summed in bfloat16 or wider, within the bound.
A program may use at most 256 MiB of HBM per device.

```python
import jax
import jax.numpy as jnp
from jax import lax

D = 768
HEADS = 12
HEAD_DIM = 64
FF = 3072
UNIT = 512
SLOTS = 4
CAP = 2048
TOKENS = 32768
N_BATCH = 16


length_patterns = [[4, 0, 0, 0], [2, 2, 0, 0], [2, 1, 0, 0], [1, 1, 1, 0], [2, 0, 0, 0], [1, 1, 0, 0], [1, 2, 1, 0], [1, 0, 0, 0]]


def draw_seq_len(key, part):
    key = jax.random.fold_in(key, 11)
    pick_key, full_key = jax.random.split(key)
    table = jnp.array(length_patterns, dtype=jnp.int32) * UNIT
    picks = jax.random.randint(pick_key, (N_BATCH,), 0, 8)
    chosen = jax.random.randint(full_key, (), 0, N_BATCH)
    picks = jnp.where(jnp.arange(N_BATCH) == chosen, 0, picks)
    return table[picks].astype(jnp.int32)


def levels(own_key, extent, pieces, low, top_value):
    def one(dim, parts):
        draws = jax.random.uniform(jax.random.fold_in(jax.random.fold_in(own_key, 6), dim), (parts,), jnp.float32, low / len(pieces), top_value / len(pieces))
        return jnp.repeat(jnp.exp(draws), extent[dim] // parts).reshape((-1,) + (1,) * (len(extent) - dim - 1))

    factor_of = one(*pieces[0])
    for cut in pieces[1:]:
        factor_of = factor_of * one(*cut)
    return factor_of


def noise(own_key, dims, spread, bound, cuts=(), held_as=jnp.bfloat16):
    factor_of = levels(own_key, dims, cuts, -0.22, 0.18) if cuts else 1.0
    entries = jax.random.normal(own_key, dims, jnp.float32) * spread * factor_of
    return jnp.minimum(jnp.maximum(entries, -bound), bound).astype(held_as)


def setup_inputs(seed: int = 0) -> dict:
    splits = jax.random.split(jax.random.key(seed), 16)
    block_in = noise(splits[0], (TOKENS, D), 1.0, 6.0, ((0, 32),))
    seq_len = draw_seq_len(jax.random.fold_in(splits[15], 71), 0)
    ln1_gain = jnp.clip(1.0 + 0.1 * jax.random.normal(splits[2], (D,), jnp.float32), 0.5, 1.5).astype(jnp.bfloat16)
    ln1_bias = noise(splits[3], (D,), 0.5, 3.0)
    qkv_weight = noise(splits[4], (D, 3, D), D ** -0.5, 0.21875, ((2, 2),))
    qkv_bias = noise(splits[5], (3, D), 0.5, 3.0, ((1, 2),))
    out_weight = noise(splits[6], (D, D), (D // 32) ** -0.5, 1.25, ((0, 2),))
    out_bias = noise(splits[7], (D,), 0.5, 3.0)
    ln2_gain = jnp.clip(1.0 + 0.1 * jax.random.normal(splits[8], (D,), jnp.float32), 0.5, 1.5).astype(jnp.bfloat16)
    ln2_bias = noise(splits[9], (D,), 0.5, 3.0)
    fc_weight = noise(splits[10], (D, FF), D ** -0.5, 0.21875, ((1, 2),))
    fc_bias = noise(splits[11], (FF,), 0.5, 3.0, ((0, 2),))
    proj_weight = noise(splits[12], (FF, D), FF ** -0.5, 0.109375, ((0, 2),))
    proj_bias = noise(splits[13], (D,), 0.5, 3.0)
    cotangent = noise(splits[14], (TOKENS, D), 1.0, 6.0, ((0, 32),))
    return {"block_in": block_in, "seq_len": seq_len, "ln1_gain": ln1_gain, "ln1_bias": ln1_bias, "qkv_weight": qkv_weight, "qkv_bias": qkv_bias, "out_weight": out_weight, "out_bias": out_bias, "ln2_gain": ln2_gain, "ln2_bias": ln2_bias, "fc_weight": fc_weight, "fc_bias": fc_bias, "proj_weight": proj_weight, "proj_bias": proj_bias, "cotangent": cotangent}


@jax.custom_vjp
def low(v):
    return lax.optimization_barrier(v.astype(jnp.bfloat16)).astype(jnp.float32)

@jax.custom_vjp
def low_back(v):
    return v

def low_keep(v):
    return (low(v), None)

def low_pass(kept, grad):
    return (grad,)

def back_keep(v):
    return (v, None)

def back_low(kept, grad):
    return (low(grad),)
low.defvjp(low_keep, low_pass)
low_back.defvjp(back_keep, back_low)

def segment_ids(lengths, count):
    bounds = jnp.cumsum(lengths).astype(jnp.int32)
    places = jnp.arange(count, dtype=jnp.int32)
    return lax.optimization_barrier(jnp.sum((places[:, None] >= bounds[None, :]).astype(jnp.int32), axis=1)).astype(jnp.int32)

def normalize(values):
    centred = values - lax.optimization_barrier(jnp.mean(values, axis=1, keepdims=True))
    return centred * lax.rsqrt(lax.optimization_barrier(jnp.mean(centred * centred, axis=1, keepdims=True)) + 1e-05)

def attend(queries, keys, values, segment):
    high = lax.Precision.HIGHEST
    count = keys.shape[0]
    block = min(512, count)
    places = jnp.arange(count, dtype=jnp.int32)
    scale = HEAD_DIM ** (-0.5)

    def one_block(start):
        query_rows = lax.dynamic_slice_in_dim(queries, start, block, 0)
        row_places = lax.dynamic_slice_in_dim(places, start, block)
        row_segment = lax.dynamic_slice_in_dim(segment, start, block)
        causal = places[None, :] <= row_places[:, None]
        same = row_segment[:, None] == segment[None, :]
        alone = (row_segment[:, None] < SLOTS) | (places[None, :] == row_places[:, None])
        allowed = (causal & same & alone)[None]
        scores = low_back(jnp.einsum('qhe,khe->hqk', query_rows, keys, precision=high) * scale)
        magnitude = jnp.sqrt(scores * scores + 1.0)
        largest = lax.optimization_barrier(jnp.max(jnp.where(allowed, magnitude, 0.0), axis=2, keepdims=True))
        exponent = jnp.where(allowed, jnp.exp(jnp.where(allowed, magnitude - largest, -30.0)), 0.0)
        probs = exponent / lax.optimization_barrier(jnp.sum(exponent, axis=2, keepdims=True))
        weights = low(scores / magnitude * probs)
        return jnp.einsum('hqk,khe->qhe', weights, values, precision=high)
    starts = jnp.arange(count // block, dtype=jnp.int32) * block
    result = lax.map(jax.checkpoint(one_block), starts)
    return result.reshape(count, HEADS * HEAD_DIM)

def forward(resid, segment, ln1_gain, ln1_bias, qkv_weight, qkv_bias, out_weight, out_bias, ln2_gain, ln2_bias, fc_weight, fc_bias, proj_weight, proj_bias):
    high = lax.Precision.HIGHEST
    count = resid.shape[0]
    rows_one = low(normalize(resid) * ln1_gain + ln1_bias)
    mixed = low(low_back(jnp.einsum('cd,dke->cke', rows_one, qkv_weight, precision=high) + qkv_bias))
    split = mixed.reshape(count, 3, HEADS, HEAD_DIM)
    context = low(low_back(attend(split[:, 0], split[:, 1], split[:, 2], segment)))
    middle = resid + low_back(jnp.dot(context, out_weight, precision=high)) + out_bias
    rows_two = low(normalize(middle) * ln2_gain + ln2_bias)
    pre_act = low_back(jnp.dot(rows_two, fc_weight, precision=high) + fc_bias)
    hidden = low(jax.nn.gelu(pre_act))
    return middle + low_back(jnp.dot(hidden, proj_weight, precision=high)) + proj_bias

def reference(block_in, seq_len, ln1_gain, ln1_bias, qkv_weight, qkv_bias, out_weight, out_bias, ln2_gain, ln2_bias, fc_weight, fc_bias, proj_weight, proj_bias, cotangent):
    weights = tuple((item.astype(jnp.float32) for item in (ln1_gain, ln1_bias, qkv_weight, qkv_bias, out_weight, out_bias, ln2_gain, ln2_bias, fc_weight, fc_bias, proj_weight, proj_bias)))
    inputs = block_in.astype(jnp.float32).reshape(N_BATCH, CAP, D)
    grads_in = cotangent.astype(jnp.float32).reshape(N_BATCH, CAP, D)

    def group(totals, item):
        resid, grad_out, lengths = item
        segment = segment_ids(lengths, CAP)

        def apply(resid_arg, *params):
            return forward(resid_arg, segment, *params)
        output, pull = jax.vjp(apply, resid, *weights)
        pulled = pull(grad_out)
        totals = tuple((total + term for total, term in zip(totals, pulled[1:])))
        return (totals, (output.astype(jnp.bfloat16), pulled[0].astype(jnp.bfloat16)))
    begin = tuple((jnp.zeros_like(item) for item in weights))
    totals, (outputs, input_grads) = lax.scan(group, begin, (inputs, grads_in, seq_len))
    return (outputs.reshape(TOKENS, D), input_grads.reshape(TOKENS, D), totals[0], totals[1], totals[2], totals[3], totals[4], totals[5], totals[6], totals[7], totals[8], totals[9], totals[10], totals[11])
```

```python
import functools
import math

import jax
import jax.numpy as jnp
from jax import lax
from jax.experimental import pallas as pl
from jax.experimental.pallas import tpu as pltpu
from jax.sharding import PartitionSpec as P

HEAD_DIM = 64
UNIT = 512
PIECE = 256
UNITS = 16
HALVINGS = 4
CHUNKS = 3
SPLIT = 3
SMALL_ROWS = 72
TALL = 256
STRIP = 16
LOG2E = math.log2(math.e)
MESH = pl.DeviceIdType.MESH
NN = (((1,), (0,)), ((), ()))
NT = (((1,), (1,)), ((), ()))
TN = (((0,), (0,)), ((), ()))


def dot(a, b, dims=NN):
    return lax.dot_general(a, b, dims, preferred_element_type=jnp.float32)


def head_mask(values, head):
    lane = lax.broadcasted_iota(jnp.int32, values.shape, 1)
    keep = (lane >= head * HEAD_DIM) & (lane < (head + 1) * HEAD_DIM)
    return jnp.where(keep, values, jnp.zeros_like(values))


def flipped(me, b):
    return me + (1 - 2 * lax.rem(lax.div(me, 1 << b), 2)) * (1 << b)


def landing_units(bits):
    return UNITS - (UNITS >> min(bits, HALVINGS)) + max(bits - HALVINGS, 0)


def reduction_steps(bits):
    return bits + min(bits, HALVINGS)


def order_of(bits, n):
    rest = list(range(bits - 1))
    turn = n % max(bits - 1, 1)
    return rest[turn:] + rest[:turn] + [bits - 1]


def greet(bits):
    me, core = lax.axis_index("batch"), lax.axis_index("tensor")
    barrier = pltpu.get_barrier_semaphore()
    pl.semaphore_signal(barrier, inc=1, device_id=(me, 1 - core), device_id_type=MESH)
    for b in range(bits):
        pl.semaphore_signal(
            barrier, inc=1, device_id=(flipped(me, b), core), device_id_type=MESH
        )
    pl.semaphore_wait(barrier, bits + 1)


class Reduction:
    def __init__(self, order, parts, sems, base, begin=0, end=None):
        self.order, self.parts, self.base = order, parts, base
        self.send_sems, self.recv_sems, self.keep_sems = sems
        halvings = min(len(order), HALVINGS)
        self.last = UNITS >> halvings
        self.turn = len(order)
        self.steps = [("half", i) for i in range(halvings)]
        self.steps += [("whole", i) for i in range(halvings, len(order))]
        self.steps += [("back", i) for i in reversed(range(halvings))]
        self.begin, self.end = begin, len(self.steps) if end is None else end

    def bit(self, i):
        return lax.rem(lax.div(lax.axis_index("batch"), 1 << self.order[i]), 2)

    def held(self, i):
        start = 0
        for k in range(min(i, HALVINGS)):
            start = start + self.bit(k) * (UNITS >> (k + 1))
        return start

    def slot(self, i):
        offset = 0
        for k in range(i):
            offset += (UNITS >> (k + 1)) if k < HALVINGS else self.last
        return offset

    def copies(self, k):
        kind, i = self.steps[k]
        for index, (data, landing, result) in enumerate(self.parts):
            if kind == "half":
                size = UNITS >> (i + 1)
                source = data(self.held(i) + (1 - self.bit(i)) * size, size)
                target = landing(self.slot(i), size)
            elif kind == "whole":
                source = data(self.held(i), self.last)
                target = landing(self.slot(i), self.last)
            else:
                size = UNITS >> (i + 1)
                source = target = result(self.held(i + 1), size)
                if k == self.turn:
                    source = data(self.held(i + 1), size)
            yield pltpu.make_async_remote_copy(
                src_ref=source,
                dst_ref=target,
                send_sem=self.send_sems.at[self.base + index, k],
                recv_sem=self.recv_sems.at[self.base + index, k],
                device_id=(flipped(lax.axis_index("batch"), self.order[i]), lax.axis_index("tensor")),
                device_id_type=MESH,
            )

    def keeps(self):
        start = self.held(len(self.order))
        for index, (data, _, result) in enumerate(self.parts):
            yield pltpu.make_async_copy(
                data(start, self.last), result(start, self.last), self.keep_sems.at[self.base + index]
            )

    def tick(self, k):
        if k > self.begin:
            kind, i = self.steps[k - 1]
            for copy in self.copies(k - 1):
                copy.wait()
            if k - 1 == self.turn:
                for copy in self.keeps():
                    copy.wait()
            if kind != "back":
                size = UNITS >> (i + 1) if kind == "half" else self.last
                start = self.held(i + 1)
                for data, landing, _ in self.parts:
                    own, came = data(start, size), landing(self.slot(i), size)

                    @pl.loop(0, size)
                    def _(n):
                        own[n] = (
                            own[n].astype(jnp.float32) + came[n].astype(jnp.float32)
                        ).astype(jnp.bfloat16)

        if k >= self.end:
            return
        if k == self.turn:
            for copy in self.keeps():
                copy.start()
        for copy in self.copies(k):
            copy.start()


def views(ref, *lead):
    return lambda start, size: ref.at[(*lead, pl.ds(start, size))]


def chunk_reductions(bits, proj, fc, lead, landed, land, results, base, sems, **limits):
    return [
        Reduction(
            order_of(bits, i),
            [
                (views(proj, lead, i), views(landed[0], land, i), views(results[0], lead, i)),
                (views(fc, lead, i), views(landed[1], land, i), views(results[1], lead, i)),
            ],
            sems,
            base + 2 * i,
            **limits,
        )
        for i in range(SPLIT)
    ]


def strips(rows):
    return [slice(s, s + STRIP) for s in range(0, rows, STRIP)]


def normed(values):
    centred = values - jnp.mean(values, axis=1, keepdims=True)
    rstd = lax.rsqrt(jnp.mean(centred * centred, axis=1, keepdims=True) + 1e-05)
    return centred * rstd, rstd


def norm_back(grad, values, rstd, gain):
    scaled = grad * gain
    inner = (
        scaled
        - jnp.mean(scaled, axis=1, keepdims=True)
        - values * jnp.mean(scaled * values, axis=1, keepdims=True)
    )
    return inner * rstd


def line(ref):
    return ref[...].astype(jnp.float32)[None, :]


def early_kernel(
    x_ref, x_hbm, g_hbm, outw_hbm, w_ref, gain_ref, shift_ref, bias_ref,
    mixed, y1t, x_peer, g_peer, outw_peer,
    x_land, rows_ref, send_sems, recv_sems, store_sem,
):
    wide, half = jnp.float32, jnp.bfloat16
    own = x_ref.shape[0]
    me, core = lax.axis_index("batch"), lax.axis_index("tensor")
    peer = (me, 1 - core)
    barrier = pltpu.get_barrier_semaphore()
    pl.semaphore_signal(barrier, inc=1, device_id=peer, device_id_type=MESH)
    pl.semaphore_wait(barrier, 1)
    swaps = [
        pltpu.make_async_remote_copy(
            src_ref=source, dst_ref=target, send_sem=send_sems.at[n], recv_sem=recv_sems.at[n],
            device_id=peer, device_id_type=MESH,
        )
        for n, (source, target) in enumerate(
            [(x_hbm, x_land), (outw_hbm, outw_peer), (g_hbm, g_peer)]
        )
    ]
    for swap in swaps:
        swap.start()
    gain, shift = line(gain_ref), line(shift_ref)
    local = w_ref.shape[2]

    def rows_of(source, first):
        @pl.loop(0, own // TALL)
        def _(n):
            at = pl.multiple_of(n * TALL, TALL)
            to = pl.ds(pl.multiple_of(first + at, TALL), TALL)
            for cut in strips(TALL):
                values = source[pl.ds(pl.multiple_of(at + cut.start, STRIP), STRIP), :]
                rows_ref[cut, :] = (normed(values.astype(wide))[0] * gain + shift).astype(half)
            for c in range(3):
                cols = slice(c * local, (c + 1) * local)
                result = dot(rows_ref[...], w_ref[c]) + bias_ref[c : c + 1, :].astype(wide)
                if c == 0:
                    result = result * HEAD_DIM**-0.5
                mixed[to, cols] = result.astype(half)
            y1t[:, to] = rows_ref[...].T

    rows_of(x_ref, pl.multiple_of(core * own, own))
    swaps[0].wait()
    store = pltpu.make_async_copy(x_land, x_peer, store_sem.at[0])
    store.start()
    rows_of(x_land, pl.multiple_of((1 - core) * own, own))
    store.wait()
    for swap in swaps[1:]:
        swap.wait()


def early(x, g, outw, w, gain, shift, bias):
    own, width = x.shape
    local = w.shape[2]
    vmem = pl.BlockSpec(memory_space=pltpu.VMEM)
    hbm = pl.BlockSpec(memory_space=pl.ANY)
    dma = pltpu.SemaphoreType.DMA
    shape = jax.ShapeDtypeStruct
    half = jnp.bfloat16
    return pl.pallas_call(
        early_kernel,
        in_specs=[vmem, hbm, hbm, hbm, vmem, vmem, vmem, vmem],
        out_specs=[vmem, vmem, hbm, hbm, hbm],
        out_shape=[
            shape((2 * own, 3 * local), half),
            shape((width, 2 * own), half),
            shape(x.shape, half),
            shape(g.shape, half),
            shape(outw.shape, half),
        ],
        scratch_shapes=[
            pltpu.VMEM(x.shape, half), pltpu.VMEM((TALL, width), half), dma((3,)), dma((3,)), dma((1,)),
        ],
        compiler_params=pltpu.CompilerParams(
            collective_id=2, has_side_effects=True, vmem_limit_bytes=56 * 2**20
        ),
        name="early",
    )(x, x, g, outw, w, gain, shift, bias)


SAFE = 64.0


def attend_forward_kernel(len_ref, q_ref, k_ref, v_ref, ctx_ref, lse_ref, pad_ref, vt_ref, acc_ref, top_ref, sum_ref, score_ref, ratio_ref, weight_ref):
    wide, half = jnp.float32, jnp.bfloat16
    blocks = q_ref.shape[0] // UNIT
    slots = len_ref.shape[1]

    def segment_of(b):
        segment, end = 0, 0
        for j in range(slots):
            end = end + len_ref[0, j]
            segment = segment + jnp.where(b * UNIT >= end, 1, 0)
        return segment

    row = lax.broadcasted_iota(jnp.int32, (128, 128), 0) // HEAD_DIM
    col = lax.broadcasted_iota(jnp.int32, (128, 128), 1) // HEAD_DIM
    same = jnp.where(row == col, 1.0, 0.0).astype(half)
    largest = []
    for ref in (q_ref, k_ref):
        most = jnp.zeros((1, 128), wide)
        for b in range(blocks):
            values = ref[b * UNIT : (b + 1) * UNIT, :]
            norms = dot(values * values, same)
            most = jnp.maximum(most, jnp.max(norms, axis=0, keepdims=True))
        largest.append(most)
    safe = jnp.max(largest[0] * largest[1]) <= SAFE * SAFE
    for b in range(blocks):
        rows = slice(b * UNIT, (b + 1) * UNIT)
        vt_ref[:, rows] = v_ref[rows, :].T

    def one_block(qi, bounded):
        start = pl.multiple_of(qi * UNIT, UNIT)
        query = q_ref[pl.ds(start, UNIT), :]
        turned = query.T
        blank = jnp.zeros((HEAD_DIM, UNIT), half)
        queries = [
            jnp.concatenate([turned[:HEAD_DIM], blank], axis=0),
            jnp.concatenate([blank, turned[HEAD_DIM:]], axis=0),
        ]
        segment = segment_of(qi)
        parts = UNIT // PIECE

        def tile(kj, diagonal):
            spots = []
            for sub in range(parts):
                at = pl.ds(pl.multiple_of(kj * UNIT + sub * PIECE, PIECE), PIECE)
                skip = sub * PIECE if diagonal else 0
                for h in range(2):
                    spots.append((sub * 2 + h, at, skip, h))

            def begin(n, at, skip, h):
                score_ref[n, :, skip:] = dot(k_ref[at, :], queries[h][:, skip:])

            begin(*spots[0])
            for place, (n, at, skip, h) in enumerate(spots):
                if place + 1 < len(spots):
                    begin(*spots[place + 1])
                first = diagonal and skip == 0
                head = slice(h * HEAD_DIM, (h + 1) * HEAD_DIM)
                total = top = jnp.zeros((STRIP, UNIT - skip), wide)

                def kept(size, offset):
                    if not diagonal:
                        return size
                    left = lax.broadcasted_iota(jnp.int32, size.shape, 0) + offset
                    right = lax.broadcasted_iota(jnp.int32, size.shape, 1)
                    keep = (left == right) | ((left < right) & (segment < slots))
                    return jnp.where(keep, size, -1e30)

                totals = {}
                for cut in strips(PIECE):
                    lead = cut.start // 128 * 128 if diagonal and bounded else 0
                    low = skip + lead
                    score = score_ref[n, cut, low:]
                    square = score * score + 1.0
                    inverse = lax.rsqrt(square)
                    size = kept((square * inverse) * LOG2E, cut.start - lead)
                    ratio = score * inverse
                    if bounded:
                        expo = jnp.exp2(size)
                        totals[lead] = totals[lead] + expo if lead in totals else expo
                        weight_ref[n, cut, low:] = (ratio * expo).astype(half)
                        if lead:
                            weight_ref[n, cut, skip:low] = jnp.zeros((STRIP, lead), half)
                    else:
                        top = jnp.maximum(top, size)
                        score_ref[n, cut, skip:] = size
                        ratio_ref[cut, skip:] = ratio
                for lead, part in totals.items():
                    if lead:
                        part = jnp.concatenate([jnp.zeros((STRIP, lead), wide), part], axis=1)
                    total = total + part
                if not bounded:
                    top = jnp.max(top, axis=0, keepdims=True)
                    if not first:
                        old = top_ref[h, :, skip:]
                        top = jnp.maximum(old, top)
                        fade = jnp.exp2(old - top)
                    for cut in strips(PIECE):
                        expo = jnp.exp2(score_ref[n, cut, skip:] - top)
                        total += expo
                        weight_ref[n, cut, skip:] = (ratio_ref[cut, skip:] * expo).astype(half)
                    top_ref[h, :, skip:] = top
                total = jnp.sum(total, axis=0, keepdims=True)
                part = dot(vt_ref[head, at], weight_ref[n, :, skip:])
                if first:
                    sum_ref[h] = total
                    acc_ref[head, :] = part
                elif bounded:
                    sum_ref[h, :, skip:] += total
                    acc_ref[head, skip:] += part
                else:
                    sum_ref[h, :, skip:] = sum_ref[h, :, skip:] * fade + total
                    acc_ref[head, skip:] = acc_ref[head, skip:] * fade + part

        tile(qi, True)

        @pl.loop(0, qi)
        def _(kj):
            @pl.when((segment_of(kj) == segment) & (segment < slots))
            def _():
                tile(kj, False)

        for h in range(2):
            head = slice(h * HEAD_DIM, (h + 1) * HEAD_DIM)
            total = sum_ref[h]
            acc_ref[head, :] = acc_ref[head, :] * (1.0 / total)
            lse = jnp.log2(total)
            if not bounded:
                lse = lse + top_ref[h]
            for kj in range(blocks):
                joined = (qi == kj) | ((segment_of(kj) == segment) & (segment < slots))
                lse_ref[0, h, kj : kj + 1, pl.ds(start, UNIT)] = lse + jnp.where(joined, 0.0, 1e30)
        pad_ref[0:1, pl.ds(start, UNIT)] = jnp.zeros((1, UNIT), wide) + jnp.where(
            segment < slots, 0.0, 1.0
        )
        ctx_ref[pl.ds(start, UNIT), :] = acc_ref[...].T.astype(half)

    @pl.when(safe)
    def _():
        @pl.loop(0, blocks)
        def _(qi):
            one_block(qi, True)

    @pl.when(jnp.logical_not(safe))
    def _():
        @pl.loop(0, blocks)
        def _(qi):
            one_block(qi, False)


def attend_forward(mixed, seq_len):
    count = mixed.shape[0]
    pairs = mixed.shape[1] // (3 * 128)

    def column(group):
        return pl.BlockSpec((count, 128), lambda p, seg: (0, group * pairs + p))

    return pl.pallas_call(
        attend_forward_kernel,
        grid_spec=pltpu.PrefetchScalarGridSpec(
            num_scalar_prefetch=1,
            grid=(pairs,),
            in_specs=[column(0), column(1), column(2)],
            out_specs=[
                pl.BlockSpec((count, 128), lambda p, seg: (0, p)),
                pl.BlockSpec((1, 2, count // UNIT, count), lambda p, seg: (p, 0, 0, 0)),
                pl.BlockSpec((1, count), lambda p, seg: (0, 0)),
            ],
            scratch_shapes=[
                pltpu.VMEM((128, count), jnp.bfloat16),
                pltpu.VMEM((128, UNIT), jnp.float32),
                pltpu.VMEM((2, 1, UNIT), jnp.float32),
                pltpu.VMEM((2, 1, UNIT), jnp.float32),
                pltpu.VMEM((4, PIECE, UNIT), jnp.float32),
                pltpu.VMEM((PIECE, UNIT), jnp.float32),
                pltpu.VMEM((4, PIECE, UNIT), jnp.bfloat16),
            ],
        ),
        out_shape=[
            jax.ShapeDtypeStruct((count, pairs * 128), jnp.bfloat16),
            jax.ShapeDtypeStruct((pairs, 2, count // UNIT, count), jnp.float32),
            jax.ShapeDtypeStruct((1, count), jnp.float32),
        ],
        compiler_params=pltpu.CompilerParams(vmem_limit_bytes=56 * 2**20),
        cost_estimate=pl.CostEstimate(flops=6 * 2 * 2 * 64 * 2048 * 1280, bytes_accessed=8 * 2**20, transcendentals=0),
        name="attend_forward",
    )(seq_len, mixed, mixed, mixed)


def middle_kernel(
    bits, schedule,
    ctx_ref, x_own, x_peer, g_own, g_peer, outw_own, outw_peer, outb_ref, gain_ref, shift_ref, fcw_ref, fcb_ref, projw_ref, projb_ref,
    block_out, gmid_hbm, gctx_ref, outg_ref, projp, fcp, proj_all, fc_all, small_ref,
    x_ref, g_ref, ctx_peer, middle, y2_ref, out_acc, gy_acc, proj_acc, fc_acc, bias_acc, gy_recv, out_recv,
    proj_land, fc_land, proj_zero, fc_zero, fcb_line, pre_ref, grad_ref, hidden_ref, slope_ref, sum_ref,
    load_sems, swap_send, swap_recv, send_sems, recv_sems, keep_sems,
):
    wide, half = jnp.float32, jnp.bfloat16
    count, width = g_ref.shape
    own = count // 2
    blocks = count // UNIT
    heads = ctx_ref.shape[1]
    broad = fcw_ref.shape[1] // CHUNKS
    me, core = lax.axis_index("batch"), lax.axis_index("tensor")
    peer = (me, 1 - core)
    theirs, mine = pl.multiple_of((1 - core) * own, own), pl.multiple_of(core * own, own)
    loads = [
        pltpu.make_async_copy(source, ref.at[pl.ds(start, own)], load_sems.at[n])
        for n, (source, ref, start) in enumerate(
            [(x_own, x_ref, mine), (x_peer, x_ref, theirs), (g_own, g_ref, mine), (g_peer, g_ref, theirs)]
        )
    ]
    for load in loads:
        load.start()
    sems = (send_sems, recv_sems, keep_sems)
    jobs = [
        chunk_reductions(
            bits, proj_zero, fc_zero, 0, (proj_land, fc_land), 0, (proj_all, fc_all), 0, sems
        ),
        chunk_reductions(
            bits, projp, fcp, 0, (proj_land, fc_land), 1, (proj_all, fc_all), 2 * SPLIT, sems,
            end=bits,
        ),
    ]

    def run(spot):
        for n, k in schedule.get(spot, ()):
            for job in jobs[n]:
                job.tick(k)

    def swap(n, source, target):
        return pltpu.make_async_remote_copy(
            src_ref=source, dst_ref=target, send_sem=swap_send.at[n], recv_sem=swap_recv.at[n],
            device_id=peer, device_id_type=MESH,
        )

    greet(bits)
    for b in range(blocks):
        rows = pl.ds(b * UNIT, UNIT)
        swap(b, ctx_ref.at[rows], ctx_peer.at[rows]).start()
    bias_acc[...] = jnp.zeros_like(bias_acc)
    out_acc[...] = jnp.zeros_like(out_acc)
    gy_acc[...] = jnp.zeros_like(gy_acc)
    for load in loads:
        load.wait()
    gain, shift = line(gain_ref), line(shift_ref)
    outb = line(outb_ref)
    fcb_line[...] = line(fcb_ref)

    for b in range(blocks):
        rows = pl.ds(b * UNIT, UNIT)
        swap(b, ctx_ref.at[rows], ctx_peer.at[rows]).wait()

        @pl.loop(0, UNIT // TALL)
        def _(n):
            at = pl.ds(pl.multiple_of(b * UNIT + n * TALL, TALL), TALL)
            middle[at, :] = dot(ctx_ref[at, :], outw_own[...]) + dot(
                ctx_peer[at, :], outw_peer[...]
            )
            for cut in strips(TALL):
                here = pl.ds(pl.multiple_of(b * UNIT + n * TALL + cut.start, STRIP), STRIP)
                values = x_ref[here, :].astype(wide) + middle[here, :] + outb
                middle[here, :] = values
                y2_ref[here, :] = (normed(values)[0] * gain + shift).astype(half)

    root = math.sqrt(2.0 / math.pi)

    @pl.loop(0, CHUNKS * blocks)
    def _(n):
        c, r = lax.div(n, blocks), lax.rem(n, blocks)
        for spot in schedule:
            if isinstance(spot, int):

                @pl.when(n == spot)
                def _(spot=spot):
                    run(spot)

        @pl.when(r == 0)
        def _():
            proj_acc[...] = jnp.zeros_like(proj_acc)
            fc_acc[...] = jnp.zeros_like(fc_acc)

        rows = pl.ds(pl.multiple_of(r * UNIT, UNIT), UNIT)
        cols = pl.ds(pl.multiple_of(c * broad, broad), broad)
        halves = [
            pl.ds(pl.multiple_of(r * UNIT + i * PIECE, PIECE), PIECE) for i in range(UNIT // PIECE)
        ]

        def begin(i):
            pre_ref[i] = dot(y2_ref[halves[i], :], fcw_ref[:, cols])
            grad_ref[i] = dot(g_ref[halves[i], :], projw_ref[cols, :], NT)

        begin(0)
        fcb = fcb_line[:, cols]
        for i, at in enumerate(halves):
            if i + 1 < len(halves):
                begin(i + 1)
            bias = jnp.zeros((STRIP, broad), wide)
            for cut in strips(PIECE):
                pre = pre_ref[i, cut, :] + fcb
                square = pre * pre
                bent = jnp.tanh(pre * (root + (root * 0.044715) * square))
                lift = 0.5 + 0.5 * bent
                hidden_ref[i * PIECE + cut.start : i * PIECE + cut.stop, :] = (pre * lift).astype(half)
                bend = (0.5 * root + (1.5 * root * 0.044715) * square) * (1.0 - bent * bent)
                grad_pre = (grad_ref[i, cut, :] * (lift + pre * bend)).astype(half)
                slope_ref[i * PIECE + cut.start : i * PIECE + cut.stop, :] = grad_pre
                bias += grad_pre.astype(wide)
            bias_acc[c] += jnp.sum(bias, axis=0, keepdims=True)
            cut = slice(i * PIECE, (i + 1) * PIECE)
            out_acc[at, :] += dot(hidden_ref[cut, :], projw_ref[cols, :])
            gy_acc[at, :] += dot(slope_ref[cut, :], fcw_ref[:, cols], NT)
        proj_acc[...] += dot(hidden_ref[...], g_ref[rows, :], TN)
        fc_acc[...] += dot(y2_ref[rows, :], slope_ref[...], TN)

        @pl.when(c == CHUNKS - 1)
        def _():
            x_ref[rows, :] = gy_acc[rows, :].astype(half)
            swap(blocks + r, x_ref.at[rows], gy_recv.at[rows]).start()

        def keep(proj_to, fc_to, slot):
            tall, wing = broad // UNITS, width // SPLIT
            flat = width // UNITS // SPLIT
            for i in range(SPLIT):
                for u in range(UNITS):
                    proj_to[slot, i, u] = proj_acc[
                        u * tall : (u + 1) * tall, i * wing : (i + 1) * wing
                    ].astype(half)
                    row = (u * SPLIT + i) * flat
                    fc_to[slot, i, u] = fc_acc[row : row + flat, :].astype(half)

        @pl.when((r == blocks - 1) & (c == 0))
        def _():
            keep(proj_zero, fc_zero, 0)

        @pl.when((r == blocks - 1) & (c > 0))
        def _():
            keep(projp, fcp, c - 1)

    run("sent")

    @pl.loop(0, own // TALL)
    def _(n):
        at = pl.multiple_of(n * TALL, TALL)
        y2_ref[pl.ds(at, TALL), :] = out_acc[pl.ds(theirs + at, TALL), :].astype(half)

    out_swap = swap(2 * blocks, y2_ref.at[pl.ds(0, own)], out_recv)
    out_swap.start()
    across = width // 128
    fc_acc[:, :heads] = jnp.zeros((width, heads), wide)
    sum_ref[...] = jnp.zeros_like(sum_ref)
    for b in range(count // TALL):
        at = pl.ds(b * TALL, TALL)
        if b % (UNIT // TALL) == 0:
            rows = pl.ds(b * TALL, UNIT)
            swap(blocks + b * TALL // UNIT, x_ref.at[rows], gy_recv.at[rows]).wait()
        run("back%d" % b)
        for cut in strips(TALL):
            here = slice(b * TALL + cut.start, b * TALL + cut.stop)
            grad = x_ref[here, :].astype(wide) + gy_recv[here, :].astype(wide)
            values, rstd = normed(middle[here, :])
            outer = g_ref[here, :].astype(wide)
            total = outer + norm_back(grad, values, rstd, gain)
            gy_acc[here, :] = total
            y2_ref[own + cut.start : own + cut.stop, :] = total.astype(half)
            terms = (total, grad * values, grad, outer)
            for s, term in enumerate(terms):
                sum_ref[s] += term
        gm = y2_ref[own : own + TALL, :]
        gctx_ref[at, :] = dot(gm, outw_own[...], NT).astype(half)
        fc_acc[:, :heads] += dot(gm, ctx_ref[at, :], TN)

    store = pltpu.make_async_copy(gy_acc.at[pl.ds(mine, own)], gmid_hbm, load_sems.at[0])
    store.start()
    outg_ref[...] = fc_acc[:, :heads].astype(half)
    small_ref[...] = jnp.zeros_like(small_ref)
    for i in range(4):
        total = jnp.sum(sum_ref[i], axis=0, keepdims=True)
        for n in range(across):
            small_ref[i * across + n : i * across + n + 1, :] = total[:, n * 128 : (n + 1) * 128]
    for c in range(CHUNKS):
        for n in range(broad // 128):
            row = 4 * across + c * (broad // 128) + n
            small_ref[row : row + 1, :] = bias_acc[c, :, n * 128 : (n + 1) * 128]
    out_swap.wait()
    projb = line(projb_ref)

    @pl.loop(0, own // TALL)
    def _(n):
        at = pl.ds(pl.multiple_of(n * TALL, TALL), TALL)
        from_own = pl.ds(pl.multiple_of(mine + n * TALL, TALL), TALL)
        both = out_acc[from_own, :] + out_recv[at, :].astype(wide)
        block_out[at, :] = (middle[from_own, :] + both + projb).astype(half)

    store.wait()
    run("end")


def middle_plan(bits, blocks):
    plan = {}

    def put(job, total, spots):
        for k in range(total + 1):
            spot = spots[k] if k < min(total, len(spots) - 1) else spots[-1]
            there = plan.setdefault(spot, [])
            there.insert(0 if k == 0 else len(there), (job, k))

    put(0, reduction_steps(bits), [4, 6, 7, 8, 10, 11, "sent", "back2", "end"])
    put(1, bits, [8, 10, "sent", "back3", "end"])
    return plan


def middle(bits, ctx, x, x_peer, g, g_peer, outw, outw_peer, outb, gain, shift, fcw, fcb, projw, projb):
    own, width = g.shape
    count, heads = ctx.shape
    broad = fcw.shape[1] // CHUNKS
    tall, flat, wing = broad // UNITS, width // UNITS // SPLIT, width // SPLIT
    landing, steps = landing_units(bits), reduction_steps(bits)
    half, wide = jnp.bfloat16, jnp.float32
    vmem = pl.BlockSpec(memory_space=pltpu.VMEM)
    hbm = pl.BlockSpec(memory_space=pl.ANY)
    dma = pltpu.SemaphoreType.DMA
    shape = jax.ShapeDtypeStruct
    return pl.pallas_call(
        functools.partial(middle_kernel, bits, middle_plan(bits, count // UNIT)),
        in_specs=[vmem] + [hbm] * 4 + [vmem] * 9,
        out_specs=[vmem, hbm, vmem, vmem, vmem, vmem, hbm, hbm, vmem],
        out_shape=[
            shape((own, width), half),
            shape((own, width), wide),
            shape((count, heads), half),
            shape((width, heads), half),
            shape((CHUNKS - 1, SPLIT, UNITS, tall, wing), half),
            shape((CHUNKS - 1, SPLIT, UNITS, flat, broad), half),
            shape((1, SPLIT, UNITS, tall, wing), half),
            shape((1, SPLIT, UNITS, flat, broad), half),
            shape((40, 128), wide),
        ],
        scratch_shapes=[
            pltpu.VMEM((count, width), half),
            pltpu.VMEM((count, width), half),
            pltpu.VMEM((count, heads), half),
            pltpu.VMEM((count, width), wide),
            pltpu.VMEM((count, width), half),
            pltpu.VMEM((count, width), wide),
            pltpu.VMEM((count, width), wide),
            pltpu.VMEM((broad, width), wide),
            pltpu.VMEM((width, broad), wide),
            pltpu.VMEM((CHUNKS, 1, broad), wide),
            pltpu.VMEM((count, width), half),
            pltpu.VMEM((own, width), half),
            pltpu.VMEM((2, SPLIT, landing, tall, wing), half),
            pltpu.VMEM((2, SPLIT, landing, flat, broad), half),
            pltpu.VMEM((1, SPLIT, UNITS, tall, wing), half),
            pltpu.VMEM((1, SPLIT, UNITS, flat, broad), half),
            pltpu.VMEM((1, CHUNKS * broad), wide),
            pltpu.VMEM((UNIT // PIECE, PIECE, broad), wide),
            pltpu.VMEM((UNIT // PIECE, PIECE, broad), wide),
            pltpu.VMEM((UNIT, broad), half),
            pltpu.VMEM((UNIT, broad), half),
            pltpu.VMEM((4, STRIP, width), wide),
            dma((4,)),
            dma((2 * (count // UNIT) + 1,)),
            dma((2 * (count // UNIT) + 1,)),
            dma((4 * SPLIT, steps)),
            dma((4 * SPLIT, steps)),
            dma((4 * SPLIT,)),
        ],
        compiler_params=pltpu.CompilerParams(
            collective_id=1, has_side_effects=True, vmem_limit_bytes=63 * 2**20
        ),
        name="middle",
    )(ctx, x, x_peer, g, g_peer, outw, outw_peer, outb, gain, shift, fcw, fcb, projw, projb)


def late_kernel(
    bits, schedule,
    q_ref, go_ref, ctx_ref, lse_ref, pad_ref, y1t_hbm, qkvw_hbm, projp_hbm, fcp_hbm, outg_ref,
    x_hbm, gmid_hbm, gain_ref, small_ref,
    proj_all, fc_all, pair_all, igrad, small,
    y1t, qkvw, x_ref, gmid, gmix, kt_ref, dqt_ref, dk_acc, dv_acc, dot_ref, part_own,
    part_send, part_recv, proj_part, fc_part, pair_part, proj_land, fc_land, pair_land, small_recv, pair_out,
    qt_ref, gt_ref, qm_ref, gm_ref, score_ref, dw_ref, weight_ref, slope_ref, sum_ref,
    load_sems, keep_sems, send_sems, recv_sems, pair_sems, small_send, small_got,
):
    wide, half = jnp.float32, jnp.bfloat16
    count = q_ref.shape[0]
    blocks = count // UNIT
    pairs = ctx_ref.shape[1] // 128
    sets = proj_part.shape[0]
    own = x_hbm.shape[0]
    me, core = lax.axis_index("batch"), lax.axis_index("tensor")
    peer = (me, 1 - core)

    loads = [
        pltpu.make_async_copy(source, target, load_sems.at[n])
        for n, (source, target) in enumerate(
            [
                (projp_hbm, proj_part),
                (fcp_hbm, fc_part),
                (y1t_hbm, y1t), (qkvw_hbm, qkvw), (x_hbm, x_ref), (gmid_hbm, gmid),
            ]
        )
    ]
    for load in loads:
        load.start()

    sems = (send_sems, recv_sems, keep_sems)
    jobs = []
    for c in range(sets):
        jobs.append(
            chunk_reductions(
                bits, proj_part, fc_part, c, (proj_land, fc_land), c, (proj_all, fc_all),
                2 * SPLIT * c, sems, begin=bits if c == 0 else 0,
            )
        )
    for p in range(pairs):
        jobs.append(
            [
                Reduction(
                    order_of(bits, i),
                    [tuple(views(ref, p, i) for ref in (pair_part, pair_land, pair_all))],
                    sems,
                    2 * SPLIT * sets + SPLIT * p + i,
                )
                for i in range(SPLIT)
            ]
        )

    def run(spot):
        for n, k in schedule.get(spot, ()):
            for job in jobs[n]:
                job.tick(k)

    greet(bits)
    loads[0].wait()
    loads[1].wait()
    run("start")
    loads[2].wait()

    small[0:32, :] = jnp.zeros((32, 128), wide)
    small[32:SMALL_ROWS, :] = small_ref[...]

    def columns(group, p):
        return pl.ds(pl.multiple_of((group * pairs + p) * 128, 128), 128)

    turns = blocks * (blocks + 1) // 2
    flat = pair_part.shape[3]

    def spread(p, source, cols, to):
        for u in range(UNITS):
            for i in range(SPLIT):
                row = (u * SPLIT + i) * flat
                pair_part[p, i, u, :, to] = source[row : row + flat, cols]

    @pl.loop(0, pairs * turns)
    def _(n):
        p, m = lax.div(n, turns), lax.rem(n, turns)
        qi = 0
        for b in range(1, blocks):
            qi = qi + jnp.where(m >= b * (b + 1) // 2, 1, 0)
        j = m - lax.div(qi * (qi + 1), 2)
        for spot in schedule:
            if isinstance(spot, int):

                @pl.when(n == spot)
                def _(spot=spot):
                    run(spot)

        lanes = columns(0, p)

        @pl.when(m == 0)
        def _():
            for b in range(blocks):
                rows = slice(b * UNIT, (b + 1) * UNIT)
                kt_ref[:, rows] = q_ref[rows, columns(1, p)].T
                product = (go_ref[rows, lanes].astype(wide) * ctx_ref[rows, lanes].astype(wide)).T
                for h in range(2):
                    head = slice(h * HEAD_DIM, (h + 1) * HEAD_DIM)
                    dot_ref[h, :, rows] = jnp.sum(product[head, :], axis=0, keepdims=True)

        start = pl.multiple_of(qi * UNIT, UNIT)
        here = pl.ds(start, UNIT)

        @pl.when(j == 0)
        def _():
            blank = jnp.zeros((HEAD_DIM, UNIT), half)
            for ref, turned, masked in ((q_ref, qt_ref, qm_ref), (go_ref, gt_ref, gm_ref)):
                values = ref[here, lanes]
                turn = values.T
                for h in range(2):
                    head = slice(h * HEAD_DIM, (h + 1) * HEAD_DIM)
                    rest = slice((1 - h) * HEAD_DIM, (2 - h) * HEAD_DIM)
                    turned[h, head, :] = turn[head]
                    turned[h, rest, :] = blank
                    masked[h] = head_mask(values, h)

        def tile(kj, diagonal):
            spots = []
            for sub in range(UNIT // PIECE):
                at = pl.ds(pl.multiple_of(kj * UNIT + sub * PIECE, PIECE), PIECE)
                skip = sub * PIECE if diagonal else 0
                for h in range(2):
                    spots.append((sub * 2 + h, at, skip, h))

            def begin(n, at, skip, h):
                score_ref[n, :, skip:] = dot(q_ref[at, columns(1, p)], qt_ref[h, :, skip:])
                dw_ref[n, :, skip:] = dot(q_ref[at, columns(2, p)], gt_ref[h, :, skip:])

            begin(*spots[0])
            for place, (n, at, skip, h) in enumerate(spots):
                if place + 1 < len(spots):
                    begin(*spots[place + 1])
                head = slice(h * HEAD_DIM, (h + 1) * HEAD_DIM)
                span = pl.ds(pl.multiple_of(start + skip, PIECE), UNIT - skip)
                lse = lse_ref[p, h, pl.ds(kj, 1), span]
                rowdot = dot_ref[h, :, span]
                if diagonal:
                    free = pad_ref[0:1, span] < 0.5
                for cut in strips(PIECE):
                    lead = cut.start // 128 * 128 if diagonal else 0
                    low = skip + lead
                    score = score_ref[n, cut, low:]
                    square = score * score + 1.0
                    inverse = lax.rsqrt(square)
                    size = (square * inverse) * LOG2E - lse[:, lead:]
                    if diagonal:
                        left = lax.broadcasted_iota(jnp.int32, size.shape, 0) + (cut.start - lead)
                        right = lax.broadcasted_iota(jnp.int32, size.shape, 1)
                        keep = (left == right) | ((left < right) & free[:, lead:])
                        size = jnp.where(keep, size, -1e30)
                    ratio = score * inverse
                    prob = jnp.exp2(size)
                    weight_ref[n, cut, low:] = (ratio * prob).astype(half)
                    factor = 1.0 + (inverse * inverse) * (inverse - 1.0)
                    slope_ref[n, cut, low:] = (
                        prob * (dw_ref[n, cut, low:] * factor - ratio * rowdot[:, lead:])
                    ).astype(half)
                    if lead:
                        blank = jnp.zeros((STRIP, lead), half)
                        weight_ref[n, cut, skip:low] = blank
                        slope_ref[n, cut, skip:low] = blank
                dv_new = dot(weight_ref[n, :, skip:], gm_ref[h, skip:, :])
                dk_new = dot(slope_ref[n, :, skip:], qm_ref[h, skip:, :])
                dq_new = dot(kt_ref[head, at], slope_ref[n, :, skip:])
                if diagonal and skip == 0:
                    dqt_ref[head, :] = dq_new
                else:
                    dqt_ref[head, skip:] += dq_new
                if diagonal and h == 0:
                    dk_acc[at, :] = dk_new
                    dv_acc[at, :] = dv_new
                else:
                    dk_acc[at, :] += dk_new
                    dv_acc[at, :] += dv_new

        @pl.when(j == 0)
        def _():
            tile(qi, True)

        @pl.when(j > 0)
        def _():
            tile(j - 1, False)

        @pl.when(j == qi)
        def _():
            gmix[here, lanes] = (dqt_ref[...].T * HEAD_DIM**-0.5).astype(half)

        @pl.when(m == turns - 1)
        def _():
            gmix[:, columns(1, p)] = dk_acc[...].astype(half)
            gmix[:, columns(2, p)] = dv_acc[...].astype(half)
            for g in range(3):
                block = gmix[:, columns(g, p)]
                total = jnp.zeros((STRIP, 128), wide)
                for cut in strips(count):
                    total += gmix[cut, columns(g, p)].astype(wide)
                small[pl.ds(16 + g * pairs + p, 1), :] = jnp.sum(total, axis=0, keepdims=True)
                pair_out[...] = dot(y1t[...], block).astype(half)
                spread(p, pair_out, slice(None), slice(g * 128, (g + 1) * 128))
            spread(p, outg_ref, lanes, slice(384, 512))

    run("after")
    for load in loads[3:]:
        load.wait()
    tall = 256
    theirs, mine = (1 - core) * own, core * own
    local = qkvw.shape[2]

    def back(first):
        rows = pl.ds(pl.multiple_of(first, tall), tall)
        return sum(
            dot(gmix[rows, g * local : (g + 1) * local], qkvw[g], NT) for g in range(3)
        )

    @pl.loop(0, own // tall)
    def _(r):
        at = pl.multiple_of(r * tall, tall)
        part_send[pl.ds(at, tall), :] = back(theirs + at).astype(half)

    swap = pltpu.make_async_remote_copy(
        src_ref=part_send, dst_ref=part_recv, send_sem=pair_sems.at[0], recv_sem=pair_sems.at[1],
        device_id=peer, device_id_type=MESH,
    )
    swap.start()
    run("sent")

    @pl.loop(0, own // tall)
    def _(r):
        at = pl.multiple_of(r * tall, tall)
        part_own[pl.ds(at, tall), :] = back(mine + at)

    run("own")
    swap.wait()
    gain = line(gain_ref)
    sum_ref[...] = jnp.zeros_like(sum_ref)

    for r in range(own // TALL):
        run("norm%d" % r)
        for cut in strips(TALL):
            rows = slice(r * TALL + cut.start, r * TALL + cut.stop)
            values, rstd = normed(x_ref[rows, :].astype(wide))
            grad = part_own[rows, :] + part_recv[rows, :].astype(wide)
            igrad[rows, :] = (gmid[rows, :] + norm_back(grad, values, rstd, gain)).astype(half)
            sum_ref[0] += grad * values
            sum_ref[1] += grad

    gain_sum = jnp.sum(sum_ref[0], axis=0, keepdims=True)
    bias_sum = jnp.sum(sum_ref[1], axis=0, keepdims=True)
    across = x_ref.shape[1] // 128
    for n in range(across):
        small[n : n + 1, :] = gain_sum[:, n * 128 : (n + 1) * 128]
        small[across + n : across + n + 1, :] = bias_sum[:, n * 128 : (n + 1) * 128]
    run("normed")

    for k in range(bits + 1):
        partner = peer if k == 0 else (flipped(me, k - 1), core)
        copy = pltpu.make_async_remote_copy(
            src_ref=small, dst_ref=small_recv.at[k], send_sem=small_send.at[k],
            recv_sem=small_got.at[k], device_id=partner, device_id_type=MESH,
        )
        copy.start()
        run("small%d" % k)
        copy.wait()
        if k == 0:
            small[0:16, :] += small_recv[0, 0:16, :]
        else:
            small[...] += small_recv[k]
    run("end")


def late_plan(bits, sets, pairs, turns):
    plan = {}

    def put(job, spots, begin=0):
        total = reduction_steps(bits) - begin
        for k in range(total + 1):
            spot = spots[k] if k < min(total, len(spots) - 1) else spots[-1]
            there = plan.setdefault(spot, [])
            there.insert(0 if k == 0 else len(there), (job, begin + k))

    put(0, ["start", 3, 5, 8, 12], bits)
    put(1, ["start", 5, 8, 10, 13, 16, 18, 21, 25])
    put(2, [turns, 14, 16, 18, 20, 22, 24, 26, 29])
    put(3, [2 * turns, 23, 25, 27, 29, "after", "own", "norm1", "normed"])
    put(4, ["after", "own", "norm1", "norm3", "small0", "small1", "small2", "small3", "end"])
    return plan


def late(bits, mixed, grad_context, context, lse, padded, y1t, qkvw, projp, fcp, outg, x, gmid, gain, small):
    count, width = mixed.shape[0], y1t.shape[0]
    pairs = context.shape[1] // 128
    own = x.shape[0]
    sets = CHUNKS - 1
    tall, wing = projp.shape[3:]
    flat, broad = fcp.shape[3:]
    landing, steps = landing_units(bits), reduction_steps(bits)
    blocks = count // UNIT
    parts = SPLIT * (2 * sets + pairs)
    half, wide = jnp.bfloat16, jnp.float32
    vmem = pl.BlockSpec(memory_space=pltpu.VMEM)
    hbm = pl.BlockSpec(memory_space=pl.ANY)
    dma = pltpu.SemaphoreType.DMA
    return pl.pallas_call(
        functools.partial(
            late_kernel, bits, late_plan(bits, sets, pairs, blocks * (blocks + 1) // 2)
        ),
        in_specs=[vmem, vmem, vmem, vmem, vmem, hbm, hbm, hbm, hbm, vmem, hbm, hbm, vmem, vmem],
        out_specs=[hbm, hbm, hbm, vmem, vmem],
        out_shape=[
            jax.ShapeDtypeStruct((sets, SPLIT, UNITS, tall, wing), half),
            jax.ShapeDtypeStruct((sets, SPLIT, UNITS, flat, broad), half),
            jax.ShapeDtypeStruct((pairs, SPLIT, UNITS, flat, 512), half),
            jax.ShapeDtypeStruct((own, width), half),
            jax.ShapeDtypeStruct((SMALL_ROWS, 128), wide),
        ],
        scratch_shapes=[
            pltpu.VMEM(y1t.shape, half),
            pltpu.VMEM(qkvw.shape, half),
            pltpu.VMEM(x.shape, half),
            pltpu.VMEM(gmid.shape, wide),
            pltpu.VMEM(mixed.shape, half),
            pltpu.VMEM((128, count), half),
            pltpu.VMEM((128, UNIT), wide),
            pltpu.VMEM((count, 128), wide),
            pltpu.VMEM((count, 128), wide),
            pltpu.VMEM((2, 1, count), wide),
            pltpu.VMEM((own, width), wide),
            pltpu.VMEM((own, width), half),
            pltpu.VMEM((own, width), half),
            pltpu.VMEM((sets, SPLIT, UNITS, tall, wing), half),
            pltpu.VMEM((sets, SPLIT, UNITS, flat, broad), half),
            pltpu.VMEM((pairs, SPLIT, UNITS, flat, 512), half),
            pltpu.VMEM((sets, SPLIT, landing, tall, wing), half),
            pltpu.VMEM((sets, SPLIT, landing, flat, broad), half),
            pltpu.VMEM((pairs, SPLIT, landing, flat, 512), half),
            pltpu.VMEM((bits + 1, SMALL_ROWS, 128), wide),
            pltpu.VMEM((width, 128), half),
            pltpu.VMEM((2, 128, UNIT), half),
            pltpu.VMEM((2, 128, UNIT), half),
            pltpu.VMEM((2, UNIT, 128), half),
            pltpu.VMEM((2, UNIT, 128), half),
            pltpu.VMEM((4, PIECE, UNIT), wide),
            pltpu.VMEM((4, PIECE, UNIT), wide),
            pltpu.VMEM((4, PIECE, UNIT), half),
            pltpu.VMEM((4, PIECE, UNIT), half),
            pltpu.VMEM((2, STRIP, width), wide),
            dma((6,)),
            dma((parts,)),
            dma((parts, steps)),
            dma((parts, steps)),
            dma((2,)),
            dma((bits + 1,)),
            dma((bits + 1,)),
        ],
        compiler_params=pltpu.CompilerParams(
            collective_id=0, has_side_effects=True, vmem_limit_bytes=62 * 2**20
        ),
        name="late",
    )(
        mixed, grad_context, context, lse, padded, y1t, qkvw, projp, fcp, outg, x, gmid, gain, small
    )


def finish_kernel(proj_first, proj_rest, fc_first, fc_rest, pair_ref, out_ref, small, rows_in, grads_in, rows_out, grads_out, proj, fc, qkv, outw, *lines):
    wide = jnp.float32
    pairs = pair_ref.shape[0]
    rows_out[...] = rows_in[...]
    grads_out[...] = grads_in[...]
    step, flat, broad = fc_rest.shape[2:]
    wing = proj_rest.shape[4]
    ahead = fc_first.shape[0]
    for c in range(CHUNKS):
        first = c < ahead
        proj_from, fc_from = (proj_first, fc_first) if first else (proj_rest, fc_rest)
        at = c if first else c - ahead
        for i in range(SPLIT):
            for s in range(step):
                proj[c, s, :, i * wing : (i + 1) * wing] = proj_from[at, i, s].astype(wide)
                row = (s * SPLIT + i) * flat
                fc[row : row + flat, c * broad : (c + 1) * broad] = fc_from[at, i, s].astype(wide)
    for i in range(SPLIT):
        for s in range(step):
            row = (s * SPLIT + i) * flat
            for p in range(pairs):
                for c in range(3):
                    qkv[c, row : row + flat, p * 128 : (p + 1) * 128] = pair_ref[
                        p, i, s, :, c * 128 : (c + 1) * 128
                    ].astype(wide)

    @pl.when(pl.program_id(0) == 0)
    def _():
        for p in range(pairs):
            for block in range(UNITS * SPLIT * flat // 128):
                rows = []
                for row in range(block * 128, (block + 1) * 128, flat):
                    u, i = divmod(row // flat, SPLIT)
                    rows.append(out_ref[p, i, u].astype(wide))
                outw[p * 128 : (p + 1) * 128, block * 128 : (block + 1) * 128] = jnp.concatenate(
                    rows, axis=0
                ).T
        across = proj.shape[3] // 128
        for g in range(3):
            for p in range(pairs):
                row = 16 + g * pairs + p
                lines[0][g : g + 1, p * 128 : (p + 1) * 128] = small[row : row + 1, :]
        first = 0
        for i, target in enumerate(lines[1:]):
            if i == 2:
                first = 32
            for n in range(target.shape[0] // 128):
                target[pl.ds(n * 128, 128)] = small[first + n]
            first += target.shape[0] // 128


def finish(proj_first, proj_rest, fc_first, fc_rest, pair_all, small, block_out, input_grad):
    ahead, _, _, tall, wing = proj_first.shape
    flat, broad = fc_first.shape[3:]
    width = wing * SPLIT
    high = flat * SPLIT
    pairs = pair_all.shape[0]
    step = 2
    wide = jnp.float32
    shape = jax.ShapeDtypeStruct
    rows = pl.BlockSpec((block_out.shape[0] * step // UNITS, width), lambda u: (u, 0))
    lengths = [width] * 6 + [CHUNKS * broad]
    block_out, input_grad, proj, fc, qkv, outw, *lines = pl.pallas_call(
        finish_kernel,
        grid=(UNITS // step,),
        in_specs=[
            pl.BlockSpec((ahead, SPLIT, step, tall, wing), lambda u: (0, 0, u, 0, 0)),
            pl.BlockSpec((CHUNKS - ahead, SPLIT, step, tall, wing), lambda u: (0, 0, u, 0, 0)),
            pl.BlockSpec((ahead, SPLIT, step, flat, broad), lambda u: (0, 0, u, 0, 0)),
            pl.BlockSpec((CHUNKS - ahead, SPLIT, step, flat, broad), lambda u: (0, 0, u, 0, 0)),
            pl.BlockSpec((pairs, SPLIT, step, flat, 384), lambda u: (0, 0, u, 0, 0)),
            pl.BlockSpec((pairs, SPLIT, UNITS, flat, 128), lambda u: (0, 0, 0, 0, 3)),
            pl.BlockSpec((SMALL_ROWS, 128), lambda u: (0, 0)),
            rows,
            rows,
        ],
        out_specs=[
            rows,
            rows,
            pl.BlockSpec((CHUNKS, step, tall, width), lambda u: (0, u, 0, 0)),
            pl.BlockSpec((step * high, CHUNKS * broad), lambda u: (u, 0)),
            pl.BlockSpec((3, step * high, pairs * 128), lambda u: (0, u, 0)),
            pl.BlockSpec((pairs * 128, width), lambda u: (0, 0)),
            pl.BlockSpec((3, pairs * 128), lambda u: (0, 0)),
        ]
        + [pl.BlockSpec((length,), lambda u: (0,)) for length in lengths],
        out_shape=[
            shape(block_out.shape, block_out.dtype),
            shape(input_grad.shape, input_grad.dtype),
            shape((CHUNKS, UNITS, tall, width), wide),
            shape((width, CHUNKS * broad), wide),
            shape((3, width, pairs * 128), wide),
            shape((pairs * 128, width), wide),
            shape((3, pairs * 128), wide),
        ]
        + [shape((length,), wide) for length in lengths],
        compiler_params=pltpu.CompilerParams(vmem_limit_bytes=61 * 2**20),
        name="finish",
    )(proj_first, proj_rest, fc_first, fc_rest, pair_all, pair_all, small, block_out, input_grad)
    return block_out, input_grad, proj.reshape(-1, width), fc, jnp.transpose(qkv, (1, 0, 2)), outw, lines


def on_device(
    block_in, seq_len, ln1_gain, ln1_bias, qkv_weight, qkv_bias, out_weight, out_bias,
    ln2_gain, ln2_bias, fc_weight, fc_bias, proj_weight, proj_bias, cotangent,
):
    bits = lax.axis_size("batch").bit_length() - 1
    qkv = jnp.transpose(qkv_weight, (1, 0, 2))
    mixed, y1t, x_peer, g_peer, outw_peer = early(
        block_in, cotangent, out_weight, qkv, ln1_gain, ln1_bias, qkv_bias
    )
    context, lse, padded = attend_forward(mixed, seq_len)
    (
        block_out, grad_middle, grad_context, out_grad, proj_parts, fc_parts, proj_first, fc_first, small,
    ) = middle(
        bits, context, block_in, x_peer, cotangent, g_peer, out_weight, outw_peer,
        out_bias, ln2_gain, ln2_bias, fc_weight, fc_bias, proj_weight, proj_bias,
    )
    proj_rest, fc_rest, pair_all, input_grad, small = late(
        bits, mixed, grad_context, context, lse, padded, y1t, qkv,
        proj_parts, fc_parts, out_grad, block_in, grad_middle, ln1_gain, small,
    )
    block_out, input_grad, proj_grad, fc_grad, qkv_grad, outw_grad, lines = finish(
        proj_first, proj_rest, fc_first, fc_rest, pair_all, small, block_out, input_grad
    )
    (
        qkv_bias_grad, gain_one_grad, shift_one_grad, out_bias_grad, gain_two_grad, shift_two_grad,
        proj_bias_grad, fc_bias_grad,
    ) = lines
    return (
        block_out,
        input_grad,
        gain_one_grad,
        shift_one_grad,
        qkv_grad,
        qkv_bias_grad,
        outw_grad,
        out_bias_grad,
        gain_two_grad,
        shift_two_grad,
        fc_grad,
        fc_bias_grad,
        proj_grad,
        proj_bias_grad,
    )


def solution(mesh):
    placed = (
        P(("batch", "tensor"), None),
        P("batch", None),
        P(),
        P(),
        P(None, None, "tensor"),
        P(None, "tensor"),
        P("tensor", None),
        P(),
        P(),
        P(),
        P(None, "tensor"),
        P("tensor"),
        P("tensor", None),
        P(),
        P(("batch", "tensor"), None),
    )
    return jax.shard_map(
        on_device,
        mesh=mesh,
        in_specs=placed,
        out_specs=(
            P(("batch", "tensor"), None),
            P(("batch", "tensor"), None),
            P(),
            P(),
            P(None, None, "tensor"),
            P(None, "tensor"),
            P("tensor", None),
            P(),
            P(),
            P(),
            P(None, "tensor"),
            P("tensor"),
            P("tensor", None),
            P(),
        ),
        check_vma=False,
    )
```
